128 devices in a mesh: fsdp: 32 (over x, y, core), adapter: 4 (over z).
Axes of the slice: x: 4, y: 4, z: 4, core: 2. Of those that a mesh axis runs over, the one named last changes fastest.
Arguments:
- hidden: bfloat16 [16384, 14336], P('fsdp', 'adapter'), may hold values from -6 to 6
- down_weight: bfloat16 [14336, 4096], P('adapter', 'fsdp'), may hold values from -0.046875 to 0.046875
- tile_adapter_choice: int32 [128, 1], P('fsdp'), may hold values from 0 to 3; in each aligned block of 4 rows (0 to 3, 4 to 7, ...) at most 2 rows name the same one
- adapter_ranks: int32 [128], P('fsdp'), may hold values from 16 to 256, as said below
- adapter_down_matrices: bfloat16 [128, 14336, 256], P(('fsdp', 'adapter')), may hold values from -0.046875 to 0.046875
- adapter_up_matrices: bfloat16 [128, 4096, 256], P(('fsdp', 'adapter')), may hold values from -0.375 to 0.375
Outputs:
- adapted: bfloat16 [16384, 4096], P('fsdp', 'adapter')
The draws below stay inside these ranges and needn't reach their ends.
Inputs may be any that keep to these rules, and one draw needn't show every extreme that they name: `tile_adapter_choice`: adapter k of fsdp index g is global adapter g * 4 + k; among the 4 tiles of one fsdp index no adapter is named by more than 2 tiles. `adapter_ranks`: multiples of 16; some adapter has rank 256.
All inputs are finite; a program needn't handle non-finite values.
Results may differ from the reference program's by a relative error of at most 0.015.
Values may be sent and summed in bfloat16 or wider, within the bound.
A program may use at most 128 MiB of HBM per device.

```python
import math
import jax
import jax.numpy as jnp
import numpy as np
from jax import lax

OUTPUT_FEATURES = 4096
HIDDEN_UNITS = 14336
MAXIMUM_RANK = 256
TILE_ROWS = 128
TILES = 4
CAP = 2
OWNERS = 4
ADAPTER_TOTAL = 128
TOKENS = 16384
N_TILES = 128
N_ADAPTER = 4


def draw_adapter_ranks(key, part):
    key = jax.random.fold_in(key, 11)
    first_key, second_key = jax.random.split(key)
    rank_draws = jax.random.randint(first_key, (ADAPTER_TOTAL,), 1, MAXIMUM_RANK // 16 + 1)
    position = jax.random.randint(second_key, (), 0, ADAPTER_TOTAL)
    forced = jnp.where(jnp.arange(ADAPTER_TOTAL) == position, MAXIMUM_RANK // 16, rank_draws)
    return (forced * 16).astype(jnp.int32)


def block_scale(own_key, dims, pieces, low, high):
    def one(axis_at, shards_of):
        steps = jax.random.uniform(jax.random.fold_in(jax.random.fold_in(own_key, 6), axis_at), (shards_of,), jnp.float32, low / len(pieces), high / len(pieces))
        return jnp.repeat(jnp.exp(steps), dims[axis_at] // shards_of).reshape((-1,) + (1,) * (len(dims) - axis_at - 1))

    level = one(*pieces[0])
    for cut in pieces[1:]:
        level = level * one(*cut)
    return level


def deal_out(own_key, own, number, rows, number_of, top, limit, slope):
    ranking = jax.random.permutation(own_key, number_of)
    packed, ordinary = load_shares(number_of, rows * top, limit, slope, True), load_shares(number_of, rows * top, limit, slope, False)
    places = jnp.arange(number_of)

    def named(sizes, offset_by):
        used = int((sizes > 0).sum())
        fixed = max(1, used // 4)
        moved = fixed + (places - fixed + offset_by * (used - fixed)) % max(1, number_of - fixed)
        return jnp.zeros((number_of,), jnp.int32).at[ranking[jnp.where(places < fixed, places, moved)]].set(jnp.asarray(sizes, jnp.int32))

    sizes = jnp.where(number % 4 == 0, named(packed, number // 4), named(ordinary, number - number // 4 - 1))
    mixed = jax.random.permutation(jax.random.fold_in(own, 3), number_of)
    source_of, receiver = mixed[0:number_of // 2 * 2:2], mixed[1:number_of // 2 * 2:2]
    slack = jnp.minimum(sizes[source_of] - 1, limit - sizes[receiver]) // 2
    slack = jnp.where((source_of == ranking[0]) | (receiver == ranking[0]) | (sizes[receiver] == 0), 0, jnp.maximum(slack, 0))
    moved = jax.random.randint(jax.random.fold_in(own, 4), (number_of // 2,), 0, 1 << 20) % (slack + 1)
    sizes = sizes.at[source_of].add(-moved).at[receiver].add(moved)
    members = jnp.searchsorted(jnp.cumsum(sizes), jnp.arange(rows * top), side="right").astype(jnp.int32)
    table = members.reshape(top, rows).T
    table = table[jax.random.permutation(jax.random.fold_in(own, 1), rows)]
    offset_by = jax.random.randint(jax.random.fold_in(own, 2), (rows, 1), 0, top)
    return jnp.take_along_axis(table, (jnp.arange(top)[None, :] + offset_by) % top, axis=1)


def load_shares(number_of, total, reach, skew, full):
    portions = [(1 << 20) // math.isqrt(standing ** skew) + 1 for standing in range(1, number_of + 1)]
    largest = reach if full else min(reach, max(-(-total // number_of), total * portions[0] // sum(portions)))
    least = 1 if total - largest >= number_of - 1 else 0
    holding, surplus = [largest] + [least] * (number_of - 1), total - largest - least * (number_of - 1)
    while surplus > 0:
        free = [i for i in range(1, number_of) if holding[i] < largest] or [i for i in range(1, number_of) if holding[i] < reach]
        whole, left = sum([portions[i] for i in free]), surplus
        for i in free:
            extra = min(reach - holding[i], max(1, left * portions[i] // whole), surplus)
            holding[i] = holding[i] + extra
            surplus = surplus - extra
    return np.array(holding)


def noise(own_key, extent, width, bound, pieces=(), dtype=jnp.bfloat16):
    level = block_scale(own_key, extent, pieces, -0.22, 0.18) if pieces else 1.0
    array = jax.random.normal(own_key, extent, jnp.float32) * width * level
    return jnp.minimum(jnp.maximum(array, -bound), bound).astype(dtype)


def setup_inputs(seed: int = 0) -> dict:
    key_list = jax.random.split(jax.random.key(seed), 7)
    hidden = noise(key_list[0], (TOKENS, HIDDEN_UNITS), 1.0, 6.0, ((0, 32), (1, 4)))
    down_weight = noise(key_list[1], (HIDDEN_UNITS, OUTPUT_FEATURES), HIDDEN_UNITS ** -0.5, 0.046875, ((0, 4), (1, 32)))
    tile_adapter_choice_keys = jax.random.split(jax.random.fold_in(key_list[2], 1), N_TILES // TILES)
    tile_adapter_choice_turns = jax.random.permutation(jax.random.fold_in(key_list[2], 3), N_TILES // TILES)
    tile_adapter_choice = jax.vmap(lambda own, number: deal_out(jax.random.fold_in(key_list[2], 2), own, number, TILES, OWNERS, 1, CAP, 2))(tile_adapter_choice_keys, tile_adapter_choice_turns).reshape((N_TILES, 1))
    adapter_ranks = draw_adapter_ranks(jax.random.fold_in(key_list[6], 71), 0)
    adapter_down_matrices = noise(key_list[4], (ADAPTER_TOTAL, HIDDEN_UNITS, MAXIMUM_RANK), HIDDEN_UNITS ** -0.5, 0.046875, ((0, 128),))
    adapter_up_matrices = noise(key_list[5], (ADAPTER_TOTAL, OUTPUT_FEATURES, MAXIMUM_RANK), MAXIMUM_RANK ** -0.5, 0.375, ((0, 128),))
    return {"hidden": hidden, "down_weight": down_weight, "tile_adapter_choice": tile_adapter_choice, "adapter_ranks": adapter_ranks, "adapter_down_matrices": adapter_down_matrices, "adapter_up_matrices": adapter_up_matrices}


adapter_alpha = 32.0


def reference(hidden, down_weight, tile_adapter_choice, adapter_ranks, adapter_down_matrices, adapter_up_matrices):
    quarter = HIDDEN_UNITS // N_ADAPTER
    base_out = jnp.zeros((TOKENS, OUTPUT_FEATURES), jnp.float32)
    for block_index in range(N_ADAPTER):
        partial_value = jnp.dot(hidden[:, block_index * quarter:(block_index + 1) * quarter],
                          down_weight[block_index * quarter:(block_index + 1) * quarter],
                          preferred_element_type=jnp.float32)
        base_out = base_out + lax.optimization_barrier(partial_value.astype(jnp.bfloat16)).astype(jnp.float32)
    tile_ids = tile_adapter_choice[:, 0].astype(jnp.int32)
    group_index = (jnp.arange(N_TILES) // TILES).astype(jnp.int32)
    adapter_index = (group_index * N_ADAPTER + tile_ids).astype(jnp.int32)
    blocks = hidden.reshape(N_TILES, TILE_ROWS, HIDDEN_UNITS)

    def tile_delta(tile_args):
        block_current, current_index = tile_args
        rank_amount = adapter_ranks[current_index]
        rank_product = jnp.dot(block_current, adapter_down_matrices[current_index], preferred_element_type=jnp.float32)
        rank_product = jnp.where(jnp.arange(MAXIMUM_RANK) < rank_amount, rank_product, 0.0).astype(jnp.bfloat16)
        complete_delta = lax.dot_general(rank_product, adapter_up_matrices[current_index], (((1,), (1,)), ((), ())),
                                     preferred_element_type=jnp.float32)
        complete_delta = complete_delta * (adapter_alpha / rank_amount.astype(jnp.float32))
        return lax.optimization_barrier(complete_delta.astype(jnp.bfloat16)).astype(jnp.float32)

    deltas = lax.map(tile_delta, (blocks, adapter_index))
    return (base_out + deltas.reshape(TOKENS, OUTPUT_FEATURES)).astype(jnp.bfloat16)
```

```python
import jax
import jax.numpy as jnp
from jax import lax
from jax.experimental import pallas as pl
from jax.experimental.pallas import tpu as pltpu
from jax.sharding import PartitionSpec as P

MESH = pl.DeviceIdType.MESH
ALPHA = 32.0
TILE = 128
TILES = 4
SLOTS = 2
N = 4
UNITS = 3584
HALF = UNITS // 2
QUART = UNITS // 4
COLS = 128
ROWS = TILES * TILE
RANK = 256
F32, BF16 = jnp.float32, jnp.bfloat16


def kernel(
    choice, ranks, h, w, a, b, out,
    held, own, sib, pack, land, a_v, b_v, part, d_send, d_recv, ring, fin_send, fin_recv, low, low_full,
    loc, w_send, w_recv, t_send, t_recv, s_send, s_recv, r_send, r_recv,
):
    f, z = lax.axis_index("fsdp"), lax.axis_index("adapter")
    x, y, c = f // 8, (f // 2) % N, f % 2

    def at(dx, dy):
        return (((x + dx + N) % N) * N + (y + dy + N) % N) * 2 + c, z

    def along(dz):
        return f, (z + dz + N) % N

    def blk(dx, dy):
        return ((x + dx + N) % N) * N + (y + dy + N) % N

    other = (x * N + y) * 2 + (1 - c), z
    me = blk(0, 0)

    own_copy = pltpu.make_async_copy(h, own, loc.at[0])
    own_copy.start()
    w_copy = pltpu.make_async_copy(w, held.at[me], loc.at[1])
    w_copy.start()
    a_copy = pltpu.make_async_copy(a, a_v, loc.at[2])
    a_copy.start()
    b_copy = pltpu.make_async_copy(b, b_v, loc.at[3])
    b_copy.start()

    barrier = pltpu.get_barrier_semaphore()
    friends = [at(1, 0), at(-1, 0), at(0, 1), at(0, -1), along(1), along(2), along(3), other]
    for friend in friends:
        pl.semaphore_signal(barrier, inc=1, device_id=friend, device_id_type=MESH)
    pl.semaphore_wait(barrier, len(friends))

    sent = []

    def remote(src, dst, s, r, device):
        copy = pltpu.make_async_remote_copy(
            src_ref=src, dst_ref=dst, send_sem=s, recv_sem=r, device_id=device, device_id_type=MESH
        )
        copy.start()
        sent.append(copy)
        return copy

    copies = {}

    def rows_of(way, piece):
        if piece is None:
            return pl.ds(way * HALF, HALF)
        return pl.ds(way * HALF + piece * QUART, QUART)

    def place(way, first, second):
        return (first, second) if way == 0 else (second, first)

    def push(key, way, origin, piece, step, source=None):
        spot = held.at[blk(*place(way, *origin)), rows_of(way, piece)]
        i = len(copies)
        copies[key] = remote(
            spot if source is None else source.at[rows_of(way, piece)],
            spot, w_send.at[i], w_recv.at[i], at(*place(way, *step)),
        )

    signs = (1, -1)
    for way in (0, 1):
        for sign in signs:
            push((1, way, sign), way, (0, 0), None, (sign, 0), w)
    for way in (0, 1):
        for sign in signs:
            push((3, way, 0, sign), way, (0, 0), None, (0, sign), w)

    sib_copy = remote(h, sib, s_send.at[0], s_recv.at[0], other)

    def slot_tile(holder, s):
        seen, found = jnp.int32(0), jnp.int32(0)
        for t in range(TILES):
            hit = (choice[t] == holder).astype(jnp.int32)
            found = found + jnp.where(seen == s, hit * t, 0)
            seen = seen + hit
        return found

    own_copy.wait()
    tiles = []
    for d in (2, 1, 3):
        holder = (z + d) % N
        for s in range(SLOTS):
            pack[d - 1, s] = own[slot_tile(holder, s)]
            tiles.append((d, s, remote(
                pack.at[d - 1, s], land.at[d - 1, s], t_send.at[d - 1, s], t_recv.at[d - 1, s], along(d)
            )))

    def multiply(first, second):
        both = jnp.concatenate([held[first], held[second]], axis=1)
        for rows, top in ((own, 0), (sib, ROWS)):
            r = jnp.dot(rows[...].reshape(ROWS, UNITS), both, preferred_element_type=F32).astype(BF16)
            part[first, pl.ds(top, ROWS)] = r[:, :COLS]
            part[second, pl.ds(top, ROWS)] = r[:, COLS:]

    def forward(way, o, sign):
        copies[(3, way, o, sign)].wait_recv()
        push((4, way, o, sign), way, (o, -sign), 0 if sign == 1 else 1, (0, sign))

    for way in (0, 1):
        for sign in signs:
            copies[(1, way, sign)].wait_recv()
            push((2, way, sign), way, (-sign, 0), 0 if sign == 1 else 1, (sign, 0))
    for way in (0, 1):
        for o in signs:
            for sign in signs:
                push((3, way, o, sign), way, (o, 0), None, (0, sign))
    for way in (0, 1):
        for sign in signs:
            forward(way, 0, sign)
    w_copy.wait()
    sib_copy.wait_recv()
    for way in (0, 1):
        for sign in signs:
            copies[(2, way, sign)].wait_recv()
        for sign in signs:
            push((3, way, 2, sign), way, (2, 0), None, (0, sign))
    multiply(blk(0, 0), blk(0, 1))
    for o in signs:
        for way in (0, 1):
            for sign in signs:
                forward(way, o, sign)

    @pl.loop(0, 2)
    def _(i):
        multiply(blk(2 * i - 1, 0), blk(2 * i - 1, 1))

    for way in (0, 1):
        for sign in signs:
            copies[(4, way, 0, sign)].wait_recv()
    multiply(blk(0, 3), blk(0, 2))

    for way in (0, 1):
        for sign in signs:
            forward(way, 2, sign)

    a_copy.wait()
    mine = [slot_tile(z, s) for s in range(SLOTS)]
    a_own = a_v[pl.ds(pl.multiple_of(z * UNITS, UNITS), UNITS)]
    for s in range(SLOTS):
        low[s] = jnp.dot(own[mine[s]], a_own, preferred_element_type=F32)

    for way in (0, 1):
        for o in (1, -1, 2):
            for sign in signs:
                copies[(4, way, o, sign)].wait_recv()

    @pl.loop(0, 4)
    def _(i):
        dx = jnp.where(i < 2, 2 * i - 1, 2)
        dy = jnp.where(i == 2, 0, 2)
        multiply(blk(dx, dy), blk(dx, dy + 1))

    for d in (1, 3, 2):
        for dd, s, copy in tiles:
            if dd == d:
                copy.wait_recv()
        source = (z - d + N) % N
        a_part = a_v[pl.ds(pl.multiple_of(source * UNITS, UNITS), UNITS)]
        r = jnp.dot(
            land[d - 1].reshape(SLOTS * TILE, UNITS), a_part, preferred_element_type=F32
        )
        for s in range(SLOTS):
            low[s] = low[s] + r[s * TILE:(s + 1) * TILE]

    rank = ranks[z]
    scale = ALPHA / rank.astype(F32)
    valid = lax.broadcasted_iota(jnp.int32, (TILE, RANK), 1) < rank
    for t in range(TILES):
        slot = jnp.int32(0)
        for before in range(t):
            slot = slot + (choice[before] == choice[t]).astype(jnp.int32)
        slot = jnp.minimum(slot, SLOTS - 1)
        keep = jnp.logical_and(valid, jnp.full((TILE, RANK), choice[t], jnp.int32) == z)
        low_full[pl.ds(t * TILE, TILE)] = jnp.where(keep, low[slot], 0.0).astype(BF16)

    b_copy.wait()

    def delta(q):
        @pl.loop(0, N)
        def _(k):
            at_rows = pl.ds(pl.multiple_of((q * N + k) * 2 * COLS, 2 * COLS), 2 * COLS)
            r = lax.dot_general(
                low_full[...], b_v[at_rows], (((1,), (1,)), ((), ())), preferred_element_type=F32
            ) * scale
            r = r.astype(BF16).astype(F32)
            even = jnp.full((ROWS, COLS), c, jnp.int32) == 0
            here = jnp.where(even, r[:, :COLS], r[:, COLS:])
            there = jnp.where(even, r[:, COLS:], r[:, :COLS])
            spot = part.at[q * N + k, pl.ds(0, ROWS)]
            spot[...] = (spot[...].astype(F32) + here).astype(BF16)
            d_send[q, k] = there.astype(BF16)

    def exchange(q, i):
        return remote(d_send.at[q], d_recv.at[q], s_send.at[1 + i], s_recv.at[1 + i], other)

    def take(q, copy):
        copy.wait_recv()

        @pl.loop(0, N)
        def _(k):
            spot = part.at[q * N + k, pl.ds(ROWS, ROWS)]
            spot[...] = (spot[...].astype(F32) + d_recv[q, k].astype(F32)).astype(BF16)

    hops = {}

    def hop(way, step, k):
        sign = 1 - 2 * way
        q = (z - sign * (1 + step) + 2 * N) % N
        spot = part.at[q * N + k, pl.ds(way * ROWS, ROWS)]
        if step:
            hops[(way, step - 1, k)].wait_recv()
            spot[...] = (spot[...].astype(F32) + ring[way, step - 1, k].astype(F32)).astype(BF16)
        hops[(way, step, k)] = remote(
            spot, ring.at[way, step, k], r_send.at[way, step, k], r_recv.at[way, step, k], along(sign)
        )

    below, above, far = (z + N - 1) % N, (z + 1) % N, (z + 2) % N
    delta(below)
    swap_below = exchange(below, 0)
    for k in range(N):
        hop(0, 0, k)
    delta(above)
    swap_above = exchange(above, 1)
    take(above, swap_above)
    for k in range(N):
        hop(1, 0, k)
    delta(far)
    swap_far = exchange(far, 2)
    delta(z)
    swap_own = exchange(z, 3)
    take(far, swap_far)
    for k in range(N):
        hop(0, 1, k)
        hop(1, 1, k)
    take(below, swap_below)
    take(z, swap_own)
    for k in range(N):
        hop(0, 2, k)
        hop(1, 2, k)
    last = []
    for k in range(N):
        for way in (1, 0):
            hops[(way, 2, k)].wait_recv()
            r = part[z * N + k, pl.ds(way * ROWS, ROWS)].astype(F32) + ring[way, 2, k].astype(F32)
            if way:
                fin_send[k] = r.astype(BF16)
                last.append(remote(fin_send.at[k], fin_recv.at[k], s_send.at[5 + k], s_recv.at[5 + k], other))
            else:
                out[:, pl.ds(pl.multiple_of((2 * k + c) * COLS, COLS), COLS)] = r.astype(BF16)
    for k in range(N):
        last[k].wait_recv()
        out[:, pl.ds(pl.multiple_of((2 * k + 1 - c) * COLS, COLS), COLS)] = fin_recv[k]
    for copy in sent:
        copy.wait_send()


def on_device(hidden, down_weight, choice, ranks, down, up):
    anywhere = pl.BlockSpec(memory_space=pl.ANY)
    small = pl.BlockSpec(memory_space=pltpu.SMEM)
    tiles = hidden.reshape(TILES, TILE, UNITS)
    dma = pltpu.SemaphoreType.DMA
    return pl.pallas_call(
        kernel,
        out_shape=jax.ShapeDtypeStruct((ROWS, N * 2 * COLS), BF16),
        in_specs=[small, small, anywhere, anywhere, anywhere, anywhere],
        out_specs=pl.BlockSpec(memory_space=pltpu.VMEM),
        scratch_shapes=[
            pltpu.VMEM((N * N, UNITS, COLS), BF16),
            pltpu.VMEM((TILES, TILE, UNITS), BF16),
            pltpu.VMEM((TILES, TILE, UNITS), BF16),
            pltpu.VMEM((N - 1, SLOTS, TILE, UNITS), BF16),
            pltpu.VMEM((N - 1, SLOTS, TILE, UNITS), BF16),
            pltpu.VMEM((N * UNITS, RANK), BF16),
            pltpu.VMEM((N * N * 2 * COLS, RANK), BF16),
            pltpu.VMEM((N * N, 2 * ROWS, COLS), BF16),
            pltpu.VMEM((N, N, ROWS, COLS), BF16),
            pltpu.VMEM((N, N, ROWS, COLS), BF16),
            pltpu.VMEM((2, 3, N, ROWS, COLS), BF16),
            pltpu.VMEM((N, ROWS, COLS), BF16),
            pltpu.VMEM((N, ROWS, COLS), BF16),
            pltpu.VMEM((SLOTS, TILE, RANK), F32),
            pltpu.VMEM((ROWS, RANK), BF16),
            dma((4,)),
            dma((40,)),
            dma((40,)),
            dma((N - 1, SLOTS)),
            dma((N - 1, SLOTS)),
            dma((9,)),
            dma((9,)),
            dma((2, 3, N)),
            dma((2, 3, N)),
        ],
        compiler_params=pltpu.CompilerParams(
            collective_id=0, has_side_effects=True, vmem_limit_bytes=62 * 2**20
        ),
        cost_estimate=pl.CostEstimate(
            flops=20_000_000_000, bytes_accessed=15_000_000, transcendentals=0
        ),
    )(choice.reshape(TILES), ranks, tiles, down_weight, down[0], up[0])


def solution(mesh):
    return jax.shard_map(
        on_device,
        mesh=mesh,
        in_specs=(
            P("fsdp", "adapter"),
            P("adapter", "fsdp"),
            P("fsdp", None),
            P("fsdp"),
            P(("fsdp", "adapter"), None, None),
            P(("fsdp", "adapter"), None, None),
        ),
        out_specs=P("fsdp", "adapter"),
        check_vma=False,
    )
```

```python
import functools

import jax
import jax.numpy as jnp
import numpy as np
from jax import lax
from jax.experimental import pallas as pl
from jax.experimental.pallas import tpu as pltpu
from jax.sharding import PartitionSpec as P

MESH = pl.DeviceIdType.MESH
ALPHA = 32.0
TILE = 128
TILES = 4
SLOTS = 2
N = 4
UNITS = 3584
HALF = UNITS // 2
QUART = UNITS // 4
COLS = 128
ROWS = TILES * TILE
RANK = 256
PARTS = QUART // COLS
STEPS = 10
LAG = 2
WIDTH = 4 * STEPS + 2
F32, BF16 = jnp.float32, jnp.bfloat16

CLASSES = (
    ((1, 1, 1, 1), {0: 3, 1: 2, 2: 1, 3: 0}, ()),
    ((2, 2, 0, 0), {}, ((0, 2, 3, 3), (1, 3, 2, 2))),
    ((2, 0, 2, 0), {0: 1, 2: 3}, ((0, 1, 1, 1), (2, 3, 3, 3))),
    ((2, 1, 1, 0), {0: 3, 1: 2, 2: 1}, ((0, 3, 3, 3),)),
    ((2, 0, 1, 1), {0: 1, 2: 3, 3: 2}, ((0, 1, 1, 1),)),
    ((2, 1, 0, 1), {1: 2, 3: 2}, ((0, 2, 1, 3),)),
)
TILE_KIND, MATRIX_KIND, PASS_ON = 64, 128, 256


@functools.cache
def routes():
    table = np.zeros(81 + len(CLASSES) * N * WIDTH, np.int32)
    for index, (counts, via, moved) in enumerate(CLASSES):
        for turn in reversed(range(N)):
            code = 0
            for i in range(N):
                code = code * 3 + counts[(i - turn) % N]
            table[code] = index * N + turn
        rows = table[81 + index * N * WIDTH:81 + (index + 1) * N * WIDTH].reshape(N, WIDTH)
        send = np.zeros((N, 2, STEPS), np.int32)
        take = np.zeros((N, 2, STEPS), np.int32)
        flows = []
        away = {(o, s) for o, s, _, _ in moved}
        for o, s, first, second in moved:
            rows[s, 4 * STEPS] = (o - s) % N
            rows[o, 4 * STEPS + 1] |= 1 << ((s - o) % N)
            for half, by in enumerate((first, second)):
                path = (o, s) if by == s else (o, by, s)
                flows.append((path, MATRIX_KIND + (s - o) % N * 8 + half * 4, MATRIX_KIND + (o - s) % N * 8 + half * 4))
        for o in range(N):
            for s in range(N):
                if s == o or (o, s) in away:
                    continue
                for slot in range(counts[o]):
                    path = (s, via[o], o) if (s - o) % N == 2 else (s, o)
                    flows.append((path, TILE_KIND + (o - s) % N * 8 + slot * 4, TILE_KIND + (s - o) % N * 8 + slot * 4))
        flows.sort(key=lambda flow: -len(flow[0]))
        for path, code_send, code_take in flows:
            link = 0 if (path[1] - path[0]) % N == 1 else 1
            for k in range(4):
                p = 0
                while send[path[0], link, p] or (len(path) == 3 and send[path[1], link, p + LAG]):
                    p += 1
                send[path[0], link, p] = code_send + k
                if len(path) == 3:
                    p += LAG
                    send[path[1], link, p] = PASS_ON
                take[path[-1], link, p] = code_take + k
        rows[:, :2 * STEPS] = send.reshape(N, -1)
        rows[:, 2 * STEPS:4 * STEPS] = take.reshape(N, -1)
    return table


def kernel(
    choice, ranks, table, h, w, a, b, out,
    held, own, sib, pool, outgo, income, b_v, part, d_own, d_send, d_recv, ring, fin_send, fin_recv,
    low, away, away_send, away_recv, low_full,
    loc, w_send, w_recv, t_send, t_recv, s_send, s_recv, f_send, f_recv, r_send, r_recv,
):
    f, z = lax.axis_index("fsdp"), lax.axis_index("adapter")
    x, y, c = f // 8, (f // 2) % N, f % 2

    def at(dx, dy):
        return (((x + dx + N) % N) * N + (y + dy + N) % N) * 2 + c, z

    def along(dz):
        return f, (z + dz + N) % N

    def blk(dx, dy):
        return ((x + dx + N) % N) * N + (y + dy + N) % N

    other = (x * N + y) * 2 + (1 - c), z
    me = blk(0, 0)

    own_copy = pltpu.make_async_copy(h, own, loc.at[0])
    own_copy.start()
    a_copies = []
    for half in range(2):
        a_copies.append(pltpu.make_async_copy(
            a.at[:, :, pl.ds(half * COLS, COLS)], pool.at[pl.ds(16 + 16 * half, 16)], loc.at[1 + half]
        ))
        a_copies[half].start()
    w_copy = pltpu.make_async_copy(w, held.at[me], loc.at[3])
    w_copy.start()

    barrier = pltpu.get_barrier_semaphore()
    friends = [at(1, 0), at(-1, 0), at(0, 1), at(0, -1), along(1), along(2), along(3), other]
    for friend in friends:
        pl.semaphore_signal(barrier, inc=1, device_id=friend, device_id_type=MESH)
    pl.semaphore_wait(barrier, len(friends))

    sent = []

    def describe(src, dst, s, r, device):
        return pltpu.make_async_remote_copy(
            src_ref=src, dst_ref=dst, send_sem=s, recv_sem=r, device_id=device, device_id_type=MESH
        )

    def remote(src, dst, s, r, device):
        copy = describe(src, dst, s, r, device)
        copy.start()
        sent.append(copy)
        return copy

    copies = {}

    def rows_of(way, piece):
        if piece is None:
            return pl.ds(way * HALF, HALF)
        return pl.ds(way * HALF + piece * QUART, QUART)

    def place(way, first, second):
        return (first, second) if way == 0 else (second, first)

    def push(key, way, origin, piece, step, source=None):
        spot = held.at[blk(*place(way, *origin)), rows_of(way, piece)]
        i = len(copies)
        copies[key] = remote(
            spot if source is None else source.at[rows_of(way, piece)],
            spot, w_send.at[i], w_recv.at[i], at(*place(way, *step)),
        )

    def forward(way, o, sign):
        copies[(3, way, o, sign)].wait_recv()
        push((4, way, o, sign), way, (o, -sign), 0 if sign == 1 else 1, (0, sign))

    signs = (1, -1)
    for way in (0, 1):
        for sign in signs:
            push((1, way, sign), way, (0, 0), None, (sign, 0), w)
    for way in (0, 1):
        for sign in signs:
            push((3, way, 0, sign), way, (0, 0), None, (0, sign), w)

    sib_copy = remote(h, sib, s_send.at[0], s_recv.at[0], other)

    def slot_tile(holder, s):
        seen, found = jnp.int32(0), jnp.int32(0)
        for t in range(TILES):
            hit = (choice[t] == holder).astype(jnp.int32)
            found = found + jnp.where(seen == s, hit * t, 0)
            seen = seen + hit
        return found

    code = jnp.int32(0)
    for o in range(N):
        count = jnp.int32(0)
        for t in range(TILES):
            count = count + (choice[t] == o).astype(jnp.int32)
        code = code * 3 + count
    found = table[code]
    base = 81 + ((found // N) * N + (z - found % N + N) % N) * WIDTH

    def fields(entry):
        return (z + entry % 64 // 8) % N, entry // 4 % 2, entry % 4

    def matrix(piece, half, k):
        return 16 + half * 16 + piece * 4 + k

    def z_copy(link, j):
        return describe(
            outgo.at[link, j], income.at[link, j], t_send.at[link, j], t_recv.at[link, j], along(1 - 2 * link)
        )

    def step(j, first):
        for link in range(2):
            entry = table[base + link * STEPS + j]
            piece, which, k = fields(entry)
            is_matrix = jnp.logical_and(entry >= MATRIX_KIND, entry < PASS_ON)
            value = pool[jnp.where(is_matrix, matrix(piece, which, k), slot_tile(piece, which) * 4 + k)]
            if not first:
                value = lax.select(entry == PASS_ON, income[link, j - LAG], value)
            outgo[link, j] = value
            z_copy(link, j).start()

    def wide(piece):
        return jnp.concatenate([piece[i * COLS:(i + 1) * COLS] for i in range(PARTS)], axis=1)

    def matrix_rows(piece, k):
        return jnp.concatenate([pool[matrix(piece, half, k)] for half in range(2)], axis=1)

    def use(j):
        for link in range(2):
            entry = table[base + (2 + link) * STEPS + j]
            piece, which, k = fields(entry)
            got = income[link, j]
            r = jnp.dot(wide(got), matrix_rows(piece, k), preferred_element_type=F32)
            for s in range(SLOTS):
                ok = jnp.logical_and(entry // 64 == 1, which == s)
                low[s] = low[s] + lax.select(ok, r, jnp.zeros_like(r))
            rows = jnp.concatenate([wide(pool[slot_tile(piece, s) * 4 + k]) for s in range(SLOTS)], axis=0)
            r = jnp.dot(rows, got, preferred_element_type=F32)
            for half in range(2):
                ok = jnp.logical_and(entry // 64 == 2, which == half)
                away[half] = away[half] + lax.select(ok, r, jnp.zeros_like(r))

    def exchange(lo, hi):
        @pl.loop(lo, hi)
        def _(j):
            for link in range(2):
                z_copy(link, j - LAG).wait_recv()
            step(j, False)
            use(j - LAG)

    def multiply(first, second):
        both = jnp.concatenate([held[first], held[second]], axis=1)
        for rows, top in ((own, 0), (sib, ROWS)):
            r = jnp.dot(rows[...].reshape(ROWS, UNITS), both, preferred_element_type=F32).astype(BF16)
            part[first, pl.ds(top, ROWS)] = r[:, :COLS]
            part[second, pl.ds(top, ROWS)] = r[:, COLS:]

    own_copy.wait()

    @pl.loop(0, TILES)
    def _(t):
        for i in range(UNITS // COLS):
            pool[t * 4 + i // PARTS, pl.ds(i % PARTS * COLS, COLS)] = own[t, :, i * COLS:(i + 1) * COLS]

    for copy in a_copies:
        copy.wait()
    for j in range(LAG):
        step(j, True)
    b_copy = pltpu.make_async_copy(b, b_v, loc.at[4])
    b_copy.start()
    away[...] = jnp.zeros_like(away)
    low[...] = jnp.zeros_like(low)
    mine = [slot_tile(z, s) for s in range(SLOTS)]

    @pl.loop(0, 4)
    def _(k):
        rows = jnp.concatenate([wide(pool[mine[s] * 4 + k]) for s in range(SLOTS)], axis=0)
        r = jnp.dot(rows, matrix_rows(z, k), preferred_element_type=F32)
        for s in range(SLOTS):
            low[s] = low[s] + r[s * TILE:(s + 1) * TILE]

    exchange(2, 5)
    for way in (0, 1):
        for sign in signs:
            copies[(1, way, sign)].wait_recv()
            push((2, way, sign), way, (-sign, 0), 0 if sign == 1 else 1, (sign, 0))
    for way in (0, 1):
        for o in signs:
            for sign in signs:
                push((3, way, o, sign), way, (o, 0), None, (0, sign))
    for way in (0, 1):
        for sign in signs:
            forward(way, 0, sign)
    exchange(5, 7)
    w_copy.wait()
    sib_copy.wait_recv()
    multiply(blk(0, 0), blk(1, 0))
    exchange(7, 9)
    multiply(blk(0, 1), blk(0, -1))
    exchange(9, 10)
    for way in (0, 1):
        for sign in signs:
            copies[(2, way, sign)].wait_recv()
        for sign in signs:
            push((3, way, 2, sign), way, (2, 0), None, (0, sign))
    for j in range(STEPS - LAG, STEPS):
        for link in range(2):
            z_copy(link, j).wait_recv()
        use(j)

    for half in range(2):
        away_send[half] = away[half].astype(BF16)
    returns = [
        remote(away_send, away_recv.at[d - 1], f_send.at[d - 1], f_recv.at[d - 1], along(d)) for d in (2, 1, 3)
    ]
    for o in signs:
        for way in (0, 1):
            for sign in signs:
                forward(way, o, sign)
    multiply(blk(-1, 0), blk(1, 1))
    for copy in returns:
        copy.wait_recv()
    flags = table[base + 4 * STEPS + 1]
    for d in (1, 2, 3):
        ok = flags // (1 << (N - d)) % 2 == 1
        for s in range(SLOTS):
            for half in range(2):
                r = away_recv[d - 1, half, s * TILE:(s + 1) * TILE].astype(F32)
                spot = low.at[s, :, half * COLS:(half + 1) * COLS]
                spot[...] = spot[...] + lax.select(ok, r, jnp.zeros_like(r))

    rank = ranks[z]
    scale = ALPHA / rank.astype(F32)
    valid = lax.broadcasted_iota(jnp.int32, (TILE, RANK), 1) < rank
    for t in range(TILES):
        slot = jnp.int32(0)
        for before in range(t):
            slot = slot + (choice[before] == choice[t]).astype(jnp.int32)
        slot = jnp.minimum(slot, SLOTS - 1)
        keep = jnp.logical_and(valid, jnp.full((TILE, RANK), choice[t], jnp.int32) == z)
        low_full[pl.ds(t * TILE, TILE)] = jnp.where(keep, low[slot], 0.0).astype(BF16)

    b_copy.wait()
    swaps = []
    for q in range(N):
        @pl.loop(0, N)
        def _(k):
            at_rows = pl.ds(pl.multiple_of((q * N + k) * 2 * COLS, 2 * COLS), 2 * COLS)
            r = lax.dot_general(
                low_full[...], b_v[at_rows], (((1,), (1,)), ((), ())), preferred_element_type=F32
            ) * scale
            r = r.astype(BF16)
            d_own[q * N + k] = lax.select(c == 0, r[:, :COLS], r[:, COLS:])
            d_send[q * N + k] = lax.select(c == 0, r[:, COLS:], r[:, :COLS])

        here = pl.ds(q * N, N)
        swaps.append(remote(d_send.at[here], d_recv.at[here], s_send.at[1 + q], s_recv.at[1 + q], other))

    def role(way, dx):
        q = (x + dx + N) % N
        return ((z - q - 1) if way == 0 else (q - 1 - z)) % N

    def hop(way, block):
        b_at = blk(*block)
        return describe(
            part.at[b_at, pl.ds(way * ROWS, ROWS)], ring.at[way, b_at],
            r_send.at[way, b_at], r_recv.at[way, b_at], along(1 - 2 * way),
        )

    def finish(block):
        k = (y + block[1] + N) % N
        return describe(fin_send.at[k], fin_recv.at[k], s_send.at[5 + k], s_recv.at[5 + k], other)

    def act(way, block, turn):
        @pl.when(role(way, block[0]) == turn)
        def _():
            b_at = blk(*block)
            k = (y + block[1] + N) % N
            if turn:
                hop(way, block).wait_recv()

            @pl.loop(0, TILES)
            def _(i):
                some = pl.ds(pl.multiple_of(i * TILE, TILE), TILE)
                spot = part.at[b_at, pl.ds(pl.multiple_of(way * ROWS + i * TILE, TILE), TILE)]
                r = spot[...].astype(F32) + (d_recv if way else d_own)[b_at, some].astype(F32)
                if turn:
                    r = r + ring[way, b_at, some].astype(F32)
                r = r.astype(BF16)
                if turn < 3:
                    spot[...] = r
                elif way:
                    fin_send[k, some] = r
                else:
                    out[some, pl.ds(pl.multiple_of((2 * k + c) * COLS, COLS), COLS)] = r

            if turn < 3:
                hop(way, block).start()
            elif way:
                finish(block).start()

    order = (
        (0, 0), (1, 0), (0, 1), (0, -1), (-1, 0), (1, 1), (1, -1), (-1, 1), (-1, -1), (2, 0),
        (0, 2), (1, 2), (-1, 2), (2, 1), (2, -1), (2, 2),
    )

    def point(p):
        for turn in (3, 2, 1, 0):
            i = p - 2 * turn
            if 0 <= i < 8:
                for block in order[2 * i:2 * i + 2]:
                    for way in (1, 0):
                        act(way, block, turn)

    multiply(blk(1, -1), blk(-1, 1))
    for way in (0, 1):
        for sign in signs:
            copies[(4, way, 0, sign)].wait_recv()
    multiply(blk(-1, -1), blk(2, 0))
    for copy in swaps:
        copy.wait_recv()
    point(0)
    point(1)
    for way in (0, 1):
        for sign in signs:
            forward(way, 2, sign)
    point(2)
    point(3)
    point(4)
    for way in (0, 1):
        for o in signs:
            for sign in signs:
                copies[(4, way, o, sign)].wait_recv()
    multiply(blk(0, 2), blk(1, 2))
    point(5)
    multiply(blk(-1, 2), blk(2, 1))
    point(6)
    for way in (0, 1):
        for sign in signs:
            copies[(4, way, 2, sign)].wait_recv()
    multiply(blk(2, -1), blk(2, 2))
    for p in range(7, 14):
        point(p)
    for block in order:
        @pl.when(role(1, block[0]) == 3)
        def _():
            k = (y + block[1] + N) % N
            finish(block).wait()
            out[:, pl.ds(pl.multiple_of((2 * k + 1 - c) * COLS, COLS), COLS)] = fin_recv[k]

        for way in (0, 1):
            @pl.when(role(way, block[0]) != 3)
            def _():
                hop(way, block).wait_send()

    @pl.loop(0, STEPS)
    def _(j):
        for link in range(2):
            z_copy(link, j).wait_send()

    for copy in sent:
        copy.wait_send()


def on_device(hidden, down_weight, choice, ranks, down, up):
    anywhere = pl.BlockSpec(memory_space=pl.ANY)
    small = pl.BlockSpec(memory_space=pltpu.SMEM)
    tiles = hidden.reshape(TILES, TILE, UNITS)
    matrix = down.reshape(4 * N, QUART, RANK)
    dma = pltpu.SemaphoreType.DMA
    return pl.pallas_call(
        kernel,
        out_shape=jax.ShapeDtypeStruct((ROWS, N * 2 * COLS), BF16),
        in_specs=[small, small, small, anywhere, anywhere, anywhere, anywhere],
        out_specs=pl.BlockSpec(memory_space=pltpu.VMEM),
        scratch_shapes=[
            pltpu.VMEM((N * N, UNITS, COLS), BF16),
            pltpu.VMEM((TILES, TILE, UNITS), BF16),
            pltpu.VMEM((TILES, TILE, UNITS), BF16),
            pltpu.VMEM((48, QUART, COLS), BF16),
            pltpu.VMEM((2, STEPS, QUART, COLS), BF16),
            pltpu.VMEM((2, STEPS, QUART, COLS), BF16),
            pltpu.VMEM((N * N * 2 * COLS, RANK), BF16),
            pltpu.VMEM((N * N, 2 * ROWS, COLS), BF16),
            pltpu.VMEM((N * N, ROWS, COLS), BF16),
            pltpu.VMEM((N * N, ROWS, COLS), BF16),
            pltpu.VMEM((N * N, ROWS, COLS), BF16),
            pltpu.VMEM((2, N * N, ROWS, COLS), BF16),
            pltpu.VMEM((N, ROWS, COLS), BF16),
            pltpu.VMEM((N, ROWS, COLS), BF16),
            pltpu.VMEM((SLOTS, TILE, RANK), F32),
            pltpu.VMEM((2, SLOTS * TILE, COLS), F32),
            pltpu.VMEM((2, SLOTS * TILE, COLS), BF16),
            pltpu.VMEM((N - 1, 2, SLOTS * TILE, COLS), BF16),
            pltpu.VMEM((ROWS, RANK), BF16),
            dma((5,)),
            dma((40,)),
            dma((40,)),
            dma((2, STEPS)),
            dma((2, STEPS)),
            dma((9,)),
            dma((9,)),
            dma((N - 1,)),
            dma((N - 1,)),
            dma((2, N * N)),
            dma((2, N * N)),
        ],
        compiler_params=pltpu.CompilerParams(
            collective_id=0, has_side_effects=True, vmem_limit_bytes=63 * 2**20
        ),
        cost_estimate=pl.CostEstimate(
            flops=20_000_000_000, bytes_accessed=15_000_000, transcendentals=0
        ),
    )(choice.reshape(TILES), ranks, jnp.asarray(routes()), tiles, down_weight, matrix, up[0])


def solution(mesh):
    return jax.shard_map(
        on_device,
        mesh=mesh,
        in_specs=(
            P("fsdp", "adapter"),
            P("adapter", "fsdp"),
            P("fsdp", None),
            P("fsdp"),
            P(("fsdp", "adapter"), None, None),
            P(("fsdp", "adapter"), None, None),
        ),
        out_specs=P("fsdp", "adapter"),
        check_vma=False,
    )
```

```python
import functools

import jax
import jax.numpy as jnp
import numpy as np
from jax import lax
from jax.experimental import pallas as pl
from jax.experimental.pallas import tpu as pltpu
from jax.sharding import PartitionSpec as P

MESH = pl.DeviceIdType.MESH
ALPHA = 32.0
TILE = 128
TILES = 4
SLOTS = 2
N = 4
UNITS = 3584
HALF = UNITS // 2
QUART = UNITS // 4
COLS = 128
ROWS = TILES * TILE
RANK = 256
CHUNK = 512
CHUNKS = UNITS // CHUNK
PARTS = CHUNK // COLS
LAG = 3
STEPS = SLOTS * CHUNKS + LAG
WIDTH = 4 * STEPS + 2
F32, BF16 = jnp.float32, jnp.bfloat16

CLASSES = (
    ((1, 1, 1, 1), {0: 3, 1: 2, 2: 1, 3: 0}, ()),
    ((2, 2, 0, 0), {0: 3, 1: 2}, ((0, 3, 3, 3), (1, 2, 2, 2))),
    ((2, 0, 2, 0), {0: 1, 2: 3}, ((0, 1, 1, 1), (2, 3, 3, 3))),
    ((2, 1, 1, 0), {0: 3, 1: 2, 2: 1}, ((0, 3, 3, 3),)),
    ((2, 0, 1, 1), {0: 1, 2: 3, 3: 2}, ((0, 1, 1, 1),)),
    ((2, 1, 0, 1), {1: 2, 3: 2}, ((0, 2, 1, 3),)),
)
TILE_KIND, MATRIX_KIND, PASS_ON = 64, 128, 256


@functools.cache
def routes():
    table = np.zeros(81 + len(CLASSES) * N * WIDTH, np.int32)
    for index, (counts, via, moved) in enumerate(CLASSES):
        for turn in reversed(range(N)):
            code = 0
            for i in range(N):
                code = code * 3 + counts[(i - turn) % N]
            table[code] = index * N + turn
        rows = table[81 + index * N * WIDTH:81 + (index + 1) * N * WIDTH].reshape(N, WIDTH)
        send = np.zeros((N, 2, STEPS), np.int32)
        take = np.zeros((N, 2, STEPS), np.int32)
        flows = []
        away = {(o, s) for o, s, _, _ in moved}
        for o, s, first, second in moved:
            rows[s, 4 * STEPS] = (o - s) % N
            rows[o, 4 * STEPS + 1] |= 1 << ((s - o) % N)
            for half, by in enumerate((first, second)):
                path = (o, s) if by == s else (o, by, s)
                flows.append((path, MATRIX_KIND + (s - o) % N * 16 + half * 8, MATRIX_KIND + (o - s) % N * 16 + half * 8))
        for o in range(N):
            for s in range(N):
                if s == o or (o, s) in away:
                    continue
                for slot in range(counts[o]):
                    path = (s, via[o], o) if (s - o) % N == 2 else (s, o)
                    flows.append((path, TILE_KIND + (o - s) % N * 16 + slot * 8, TILE_KIND + (s - o) % N * 16 + slot * 8))
        flows.sort(key=lambda flow: -len(flow[0]))
        for path, code_send, code_take in flows:
            link = 0 if (path[1] - path[0]) % N == 1 else 1
            for k in range(CHUNKS):
                p = 0
                while send[path[0], link, p] or (len(path) == 3 and send[path[1], link, p + LAG]):
                    p += 1
                send[path[0], link, p] = code_send + k
                if len(path) == 3:
                    p += LAG
                    send[path[1], link, p] = PASS_ON
                take[path[-1], link, p] = code_take + k
        rows[:, :2 * STEPS] = send.reshape(N, -1)
        rows[:, 2 * STEPS:4 * STEPS] = take.reshape(N, -1)
    return table


def kernel(
    choice, ranks, table, h, w, a, b, out,
    held, own, sib, pool, outgo, income, b_v, part, d_own, d_send, d_recv, ring, fin_send, fin_recv,
    low, away, away_send, away_recv, low_full,
    loc, w_send, w_recv, t_send, t_recv, s_send, s_recv, f_send, f_recv, r_send, r_recv,
):
    f, z = lax.axis_index("fsdp"), lax.axis_index("adapter")
    x, y, c = f // 8, (f // 2) % N, f % 2

    def at(dx, dy):
        return (((x + dx + N) % N) * N + (y + dy + N) % N) * 2 + c, z

    def along(dz):
        return f, (z + dz + N) % N

    def blk(dx, dy):
        return ((x + dx + N) % N) * N + (y + dy + N) % N

    other = (x * N + y) * 2 + (1 - c), z
    me = blk(0, 0)

    own_copy = pltpu.make_async_copy(h, own, loc.at[0])
    own_copy.start()
    a_copies = []
    for half in range(2):
        a_copies.append(pltpu.make_async_copy(
            a.at[:, :, pl.ds(half * COLS, COLS)], pool.at[pl.ds((1 + half) * N * CHUNKS, N * CHUNKS)], loc.at[1 + half]
        ))
        a_copies[half].start()
    w_copy = pltpu.make_async_copy(w, held.at[me], loc.at[3])
    w_copy.start()

    barrier = pltpu.get_barrier_semaphore()
    friends = [at(1, 0), at(-1, 0), at(0, 1), at(0, -1), along(1), along(2), along(3), other]
    for friend in friends:
        pl.semaphore_signal(barrier, inc=1, device_id=friend, device_id_type=MESH)
    own_copy.wait()

    @pl.loop(0, TILES)
    def _(t):
        for i in range(UNITS // COLS):
            pool[t * CHUNKS + i // PARTS, pl.ds(i % PARTS * COLS, COLS)] = own[t, :, i * COLS:(i + 1) * COLS]

    pl.semaphore_wait(barrier, len(friends))

    sent = []

    def describe(src, dst, s, r, device):
        return pltpu.make_async_remote_copy(
            src_ref=src, dst_ref=dst, send_sem=s, recv_sem=r, device_id=device, device_id_type=MESH
        )

    def remote(src, dst, s, r, device):
        copy = describe(src, dst, s, r, device)
        copy.start()
        sent.append(copy)
        return copy

    copies = {}

    def rows_of(way, piece):
        if piece is None:
            return pl.ds(way * HALF, HALF)
        return pl.ds(way * HALF + piece * QUART, QUART)

    def place(way, first, second):
        return (first, second) if way == 0 else (second, first)

    def push(key, way, origin, piece, step, source=None):
        spot = held.at[blk(*place(way, *origin)), rows_of(way, piece)]
        i = len(copies)
        copies[key] = remote(
            spot if source is None else source.at[rows_of(way, piece)],
            spot, w_send.at[i], w_recv.at[i], at(*place(way, *step)),
        )

    def forward(way, o, sign):
        copies[(3, way, o, sign)].wait_recv()
        push((4, way, o, sign), way, (o, -sign), 0 if sign == 1 else 1, (0, sign))

    signs = (1, -1)
    for way in (0, 1):
        for sign in signs:
            push((1, way, sign), way, (0, 0), None, (sign, 0), w)
    for way in (0, 1):
        for sign in signs:
            push((3, way, 0, sign), way, (0, 0), None, (0, sign), w)

    sib_copy = remote(h, sib, s_send.at[0], s_recv.at[0], other)

    def slot_tile(holder, s):
        seen, found = jnp.int32(0), jnp.int32(0)
        for t in range(TILES):
            hit = (choice[t] == holder).astype(jnp.int32)
            found = found + jnp.where(seen == s, hit * t, 0)
            seen = seen + hit
        return found

    code = jnp.int32(0)
    for o in range(N):
        count = jnp.int32(0)
        for t in range(TILES):
            count = count + (choice[t] == o).astype(jnp.int32)
        code = code * 3 + count
    found = table[code]
    base = 81 + ((found // N) * N + (z - found % N + N) % N) * WIDTH

    def fields(entry):
        return (z + entry % 64 // 16) % N, entry // 8 % 2, jnp.minimum(entry % 8, CHUNKS - 1)

    def matrix(piece, half, k):
        return TILES * CHUNKS + (half * N + piece) * CHUNKS + k

    def z_copy(link, j):
        return describe(
            outgo.at[link, j], income.at[link, j], t_send.at[link, j], t_recv.at[link, j], along(1 - 2 * link)
        )

    def step(j, first):
        for link in range(2):
            entry = table[base + link * STEPS + j]
            piece, which, k = fields(entry)
            is_matrix = jnp.logical_and(entry >= MATRIX_KIND, entry < PASS_ON)
            value = pool[jnp.where(is_matrix, matrix(piece, which, k), slot_tile(piece, which) * CHUNKS + k)]
            if not first:
                value = lax.select(entry == PASS_ON, income[link, j - LAG], value)
            outgo[link, j] = value
            z_copy(link, j).start()

    def wide(piece):
        return jnp.concatenate([piece[i * COLS:(i + 1) * COLS] for i in range(PARTS)], axis=1)

    def matrix_rows(piece, k):
        return jnp.concatenate([pool[matrix(piece, half, k)] for half in range(2)], axis=1)

    def use(j):
        for link in range(2):
            entry = table[base + (2 + link) * STEPS + j]
            piece, which, k = fields(entry)
            got = income[link, j]
            r = jnp.dot(wide(got), matrix_rows(piece, k), preferred_element_type=F32)
            for s in range(SLOTS):
                ok = jnp.logical_and(entry // 64 == 1, which == s)
                low[s] = low[s] + lax.select(ok, r, jnp.zeros_like(r))
            rows = jnp.concatenate([wide(pool[slot_tile(piece, s) * CHUNKS + k]) for s in range(SLOTS)], axis=0)
            r = jnp.dot(rows, got, preferred_element_type=F32)
            for half in range(2):
                ok = jnp.logical_and(entry // 64 == 2, which == half)
                away[half] = away[half] + lax.select(ok, r, jnp.zeros_like(r))

    def exchange(lo, hi):
        @pl.loop(lo, hi)
        def _(j):
            for link in range(2):
                z_copy(link, j - LAG).wait_recv()
            step(j, False)
            use(j - LAG)

    def multiply(first, second):
        both = jnp.concatenate([held[first], held[second]], axis=1)
        for rows, top in ((own, 0), (sib, ROWS)):
            r = jnp.dot(rows[...].reshape(ROWS, UNITS), both, preferred_element_type=F32).astype(BF16)
            part[first, pl.ds(top, ROWS)] = r[:, :COLS]
            part[second, pl.ds(top, ROWS)] = r[:, COLS:]

    for copy in a_copies:
        copy.wait()
    for j in range(LAG):
        step(j, True)
    b_copy = pltpu.make_async_copy(b, b_v, loc.at[4])
    b_copy.start()
    away[...] = jnp.zeros_like(away)
    low[...] = jnp.zeros_like(low)
    mine = [slot_tile(z, s) for s in range(SLOTS)]

    @pl.loop(0, CHUNKS)
    def _(k):
        rows = jnp.concatenate([wide(pool[mine[s] * CHUNKS + k]) for s in range(SLOTS)], axis=0)
        r = jnp.dot(rows, matrix_rows(z, k), preferred_element_type=F32)
        for s in range(SLOTS):
            low[s] = low[s] + r[s * TILE:(s + 1) * TILE]

    exchange(LAG, 9)
    for way in (0, 1):
        for sign in signs:
            copies[(1, way, sign)].wait_recv()
            push((2, way, sign), way, (-sign, 0), 0 if sign == 1 else 1, (sign, 0))
    for way in (0, 1):
        for o in signs:
            for sign in signs:
                push((3, way, o, sign), way, (o, 0), None, (0, sign))
    for way in (0, 1):
        for sign in signs:
            forward(way, 0, sign)
    exchange(9, 11)
    w_copy.wait()
    sib_copy.wait_recv()
    multiply(blk(0, 0), blk(1, 0))
    exchange(11, 14)
    multiply(blk(0, 1), blk(0, -1))
    exchange(14, STEPS - 1)
    for link in range(2):
        z_copy(link, STEPS - 1 - LAG).wait_recv()
    use(STEPS - 1 - LAG)

    for half in range(2):
        away_send[half] = away[half].astype(BF16)
    returns = [
        remote(away_send, away_recv.at[d - 1], f_send.at[d - 1], f_recv.at[d - 1], along(d)) for d in (2, 1, 3)
    ]
    step(STEPS - 1, False)
    for way in (0, 1):
        for sign in signs:
            copies[(2, way, sign)].wait_recv()
        for sign in signs:
            push((3, way, 2, sign), way, (2, 0), None, (0, sign))
    for o in signs:
        for way in (0, 1):
            for sign in signs:
                forward(way, o, sign)
    multiply(blk(-1, 0), blk(1, 1))
    for j in range(STEPS - LAG, STEPS):
        for link in range(2):
            z_copy(link, j).wait_recv()
        use(j)
        if j == STEPS - LAG:
            multiply(blk(1, -1), blk(-1, 1))
    for copy in returns:
        copy.wait_recv()
    flags = table[base + 4 * STEPS + 1]
    for d in (1, 2, 3):
        ok = flags // (1 << (N - d)) % 2 == 1
        for s in range(SLOTS):
            for half in range(2):
                r = away_recv[d - 1, half, s * TILE:(s + 1) * TILE].astype(F32)
                spot = low.at[s, :, half * COLS:(half + 1) * COLS]
                spot[...] = spot[...] + lax.select(ok, r, jnp.zeros_like(r))

    rank = ranks[z]
    scale = ALPHA / rank.astype(F32)
    valid = lax.broadcasted_iota(jnp.int32, (TILE, RANK), 1) < rank
    for t in range(TILES):
        slot = jnp.int32(0)
        for before in range(t):
            slot = slot + (choice[before] == choice[t]).astype(jnp.int32)
        slot = jnp.minimum(slot, SLOTS - 1)
        keep = jnp.logical_and(valid, jnp.full((TILE, RANK), choice[t], jnp.int32) == z)
        low_full[pl.ds(t * TILE, TILE)] = jnp.where(keep, low[slot], 0.0).astype(BF16)

    b_copy.wait()

    def delta(i, q):
        @pl.loop(0, N)
        def _(k):
            at_rows = pl.ds(pl.multiple_of((q * N + k) * 2 * COLS, 2 * COLS), 2 * COLS)
            r = lax.dot_general(
                low_full[...], b_v[at_rows], (((1,), (1,)), ((), ())), preferred_element_type=F32
            ) * scale
            r = r.astype(BF16)
            d_own[q * N + k] = lax.select(c == 0, r[:, :COLS], r[:, COLS:])
            d_send[q * N + k] = lax.select(c == 0, r[:, COLS:], r[:, :COLS])

        here = pl.ds(q * N, N)
        return remote(d_send.at[here], d_recv.at[here], s_send.at[1 + i], s_recv.at[1 + i], other)

    def role(way, dx):
        q = (x + dx + N) % N
        return ((z - q - 1) if way == 0 else (q - 1 - z)) % N

    def hop(way, block):
        b_at = blk(*block)
        return describe(
            part.at[b_at, pl.ds(way * ROWS, ROWS)], ring.at[way, b_at],
            r_send.at[way, b_at], r_recv.at[way, b_at], along(1 - 2 * way),
        )

    def finish(block):
        k = (y + block[1] + N) % N
        return describe(fin_send.at[k], fin_recv.at[k], s_send.at[5 + k], s_recv.at[5 + k], other)

    def act(way, block, turn):
        @pl.when(role(way, block[0]) == turn)
        def _():
            b_at = blk(*block)
            k = (y + block[1] + N) % N
            if turn:
                hop(way, block).wait_recv()

            @pl.loop(0, TILES)
            def _(i):
                some = pl.ds(pl.multiple_of(i * TILE, TILE), TILE)
                spot = part.at[b_at, pl.ds(pl.multiple_of(way * ROWS + i * TILE, TILE), TILE)]
                r = spot[...].astype(F32) + (d_recv if way else d_own)[b_at, some].astype(F32)
                if turn:
                    r = r + ring[way, b_at, some].astype(F32)
                r = r.astype(BF16)
                if turn < 3:
                    spot[...] = r
                elif way:
                    fin_send[k, some] = r
                else:
                    out[some, pl.ds(pl.multiple_of((2 * k + c) * COLS, COLS), COLS)] = r

            if turn < 3:
                hop(way, block).start()
            elif way:
                finish(block).start()

    order = (
        (0, 0), (1, 0), (0, 1), (0, -1), (-1, 0), (1, 1), (1, -1), (-1, 1), (-1, -1), (2, 0),
        (0, 2), (1, 2), (-1, 2), (2, 1), (2, -1), (2, 2),
    )

    def stage(turn, blocks, ways=(1, 0)):
        for block in blocks:
            for way in ways:
                act(way, block, turn)

    early, late = order[:10], order[10:]
    swaps = [delta(0, (z + 1) % N), delta(1, (z + N - 1) % N)]
    stage(0, early[:8], (0,))
    swaps[0].wait_recv()
    stage(0, early[:8], (1,))
    for way in (0, 1):
        for sign in signs:
            copies[(4, way, 0, sign)].wait_recv()
    multiply(blk(-1, -1), blk(2, 0))
    stage(0, early[8:])
    for way in (0, 1):
        for sign in signs:
            forward(way, 2, sign)
    swaps.append(delta(2, (z + 2) % N))
    swaps.append(delta(3, z))
    for copy in swaps[1:]:
        copy.wait_recv()
    stage(1, early)
    for way in (0, 1):
        for o in signs:
            for sign in signs:
                copies[(4, way, o, sign)].wait_recv()
    multiply(blk(0, 2), blk(1, 2))
    stage(0, late[:2])
    multiply(blk(-1, 2), blk(2, 1))
    stage(0, late[2:4])
    stage(2, early)
    for way in (0, 1):
        for sign in signs:
            copies[(4, way, 2, sign)].wait_recv()
    multiply(blk(2, -1), blk(2, 2))
    stage(0, late[4:])
    stage(1, late)
    stage(3, early)
    stage(2, late)
    stage(3, late)
    for block in order:
        @pl.when(role(1, block[0]) == 3)
        def _():
            k = (y + block[1] + N) % N
            finish(block).wait()
            out[:, pl.ds(pl.multiple_of((2 * k + 1 - c) * COLS, COLS), COLS)] = fin_recv[k]

        for way in (0, 1):
            @pl.when(role(way, block[0]) != 3)
            def _():
                hop(way, block).wait_send()

    @pl.loop(0, STEPS)
    def _(j):
        for link in range(2):
            z_copy(link, j).wait_send()

    for copy in sent:
        copy.wait_send()


def on_device(hidden, down_weight, choice, ranks, down, up):
    anywhere = pl.BlockSpec(memory_space=pl.ANY)
    small = pl.BlockSpec(memory_space=pltpu.SMEM)
    tiles = hidden.reshape(TILES, TILE, UNITS)
    matrix = down.reshape(N * CHUNKS, CHUNK, RANK)
    dma = pltpu.SemaphoreType.DMA
    return pl.pallas_call(
        kernel,
        out_shape=jax.ShapeDtypeStruct((ROWS, N * 2 * COLS), BF16),
        in_specs=[small, small, small, anywhere, anywhere, anywhere, anywhere],
        out_specs=pl.BlockSpec(memory_space=pltpu.VMEM),
        scratch_shapes=[
            pltpu.VMEM((N * N, UNITS, COLS), BF16),
            pltpu.VMEM((TILES, TILE, UNITS), BF16),
            pltpu.VMEM((TILES, TILE, UNITS), BF16),
            pltpu.VMEM((3 * N * CHUNKS, CHUNK, COLS), BF16),
            pltpu.VMEM((2, STEPS, CHUNK, COLS), BF16),
            pltpu.VMEM((2, STEPS, CHUNK, COLS), BF16),
            pltpu.VMEM((N * N * 2 * COLS, RANK), BF16),
            pltpu.VMEM((N * N, 2 * ROWS, COLS), BF16),
            pltpu.VMEM((N * N, ROWS, COLS), BF16),
            pltpu.VMEM((N * N, ROWS, COLS), BF16),
            pltpu.VMEM((N * N, ROWS, COLS), BF16),
            pltpu.VMEM((2, N * N, ROWS, COLS), BF16),
            pltpu.VMEM((N, ROWS, COLS), BF16),
            pltpu.VMEM((N, ROWS, COLS), BF16),
            pltpu.VMEM((SLOTS, TILE, RANK), F32),
            pltpu.VMEM((2, SLOTS * TILE, COLS), F32),
            pltpu.VMEM((2, SLOTS * TILE, COLS), BF16),
            pltpu.VMEM((N - 1, 2, SLOTS * TILE, COLS), BF16),
            pltpu.VMEM((ROWS, RANK), BF16),
            dma((5,)),
            dma((40,)),
            dma((40,)),
            dma((2, STEPS)),
            dma((2, STEPS)),
            dma((9,)),
            dma((9,)),
            dma((N - 1,)),
            dma((N - 1,)),
            dma((2, N * N)),
            dma((2, N * N)),
        ],
        compiler_params=pltpu.CompilerParams(
            collective_id=0, has_side_effects=True, vmem_limit_bytes=63 * 2**20
        ),
        cost_estimate=pl.CostEstimate(
            flops=20_000_000_000, bytes_accessed=15_000_000, transcendentals=0
        ),
    )(choice.reshape(TILES), ranks, jnp.asarray(routes()), tiles, down_weight, matrix, up[0])


def solution(mesh):
    return jax.shard_map(
        on_device,
        mesh=mesh,
        in_specs=(
            P("fsdp", "adapter"),
            P("adapter", "fsdp"),
            P("fsdp", None),
            P("fsdp"),
            P(("fsdp", "adapter"), None, None),
            P(("fsdp", "adapter"), None, None),
        ),
        out_specs=P("fsdp", "adapter"),
        check_vma=False,
    )
```

```python
import functools

import jax
import jax.numpy as jnp
import numpy as np
from jax import lax
from jax.experimental import pallas as pl
from jax.experimental.pallas import tpu as pltpu
from jax.sharding import PartitionSpec as P

MESH = pl.DeviceIdType.MESH
ALPHA = 32.0
TILE = 128
TILES = 4
SLOTS = 2
N = 4
UNITS = 3584
HALF = UNITS // 2
QUART = UNITS // 4
COLS = 128
ROWS = TILES * TILE
RANK = 256
CHUNK = 512
CHUNKS = UNITS // CHUNK
PARTS = CHUNK // COLS
LAG = 3
STEPS = SLOTS * CHUNKS + LAG
WIDTH = 4 * STEPS + 2
F32, BF16 = jnp.float32, jnp.bfloat16

CLASSES = (
    ((1, 1, 1, 1), {0: 3, 1: 2, 2: 1, 3: 0}, ()),
    ((2, 2, 0, 0), {0: 3, 1: 2}, ((0, 3, 3, 3), (1, 2, 2, 2))),
    ((2, 0, 2, 0), {0: 1, 2: 3}, ((0, 1, 1, 1), (2, 3, 3, 3))),
    ((2, 1, 1, 0), {0: 3, 1: 2, 2: 1}, ((0, 3, 3, 3),)),
    ((2, 0, 1, 1), {0: 1, 2: 3, 3: 2}, ((0, 1, 1, 1),)),
    ((2, 1, 0, 1), {1: 2, 3: 2}, ((0, 2, 1, 3),)),
)
TILE_KIND, MATRIX_KIND, PASS_ON = 64, 128, 256


@functools.cache
def routes():
    table = np.zeros(81 + len(CLASSES) * N * WIDTH, np.int32)
    for index, (counts, via, moved) in enumerate(CLASSES):
        for turn in reversed(range(N)):
            code = 0
            for i in range(N):
                code = code * 3 + counts[(i - turn) % N]
            table[code] = index * N + turn
        rows = table[81 + index * N * WIDTH:81 + (index + 1) * N * WIDTH].reshape(N, WIDTH)
        send = np.zeros((N, 2, STEPS), np.int32)
        take = np.zeros((N, 2, STEPS), np.int32)
        flows = []
        away = {(o, s) for o, s, _, _ in moved}
        for o, s, first, second in moved:
            rows[s, 4 * STEPS] = (o - s) % N
            rows[o, 4 * STEPS + 1] |= 1 << ((s - o) % N)
            for half, by in enumerate((first, second)):
                path = (o, s) if by == s else (o, by, s)
                flows.append((path, MATRIX_KIND + (s - o) % N * 16 + half * 8, MATRIX_KIND + (o - s) % N * 16 + half * 8))
        for o in range(N):
            for s in range(N):
                if s == o or (o, s) in away:
                    continue
                for slot in range(counts[o]):
                    path = (s, via[o], o) if (s - o) % N == 2 else (s, o)
                    flows.append((path, TILE_KIND + (o - s) % N * 16 + slot * 8, TILE_KIND + (s - o) % N * 16 + slot * 8))
        flows.sort(key=lambda flow: -len(flow[0]))
        for path, code_send, code_take in flows:
            link = 0 if (path[1] - path[0]) % N == 1 else 1
            for k in range(CHUNKS):
                p = 0
                while send[path[0], link, p] or (len(path) == 3 and send[path[1], link, p + LAG]):
                    p += 1
                send[path[0], link, p] = code_send + k
                if len(path) == 3:
                    p += LAG
                    send[path[1], link, p] = PASS_ON
                take[path[-1], link, p] = code_take + k
        rows[:, :2 * STEPS] = send.reshape(N, -1)
        rows[:, 2 * STEPS:4 * STEPS] = take.reshape(N, -1)
    return table


def kernel(
    choice, ranks, table, h, w, a, b, out,
    held, own, sib, pool, outgo, income, b_v, part, d_own, d_send, d_recv, ring, fin_send, fin_recv,
    low, away, away_send, away_recv, low_full,
    loc, w_send, w_recv, t_send, t_recv, s_send, s_recv, f_send, f_recv, r_send, r_recv,
):
    f, z = lax.axis_index("fsdp"), lax.axis_index("adapter")
    x, y, c = f // 8, (f // 2) % N, f % 2

    def at(dx, dy):
        return (((x + dx + N) % N) * N + (y + dy + N) % N) * 2 + c, z

    def along(dz):
        return f, (z + dz + N) % N

    def blk(dx, dy):
        return ((x + dx + N) % N) * N + (y + dy + N) % N

    other = (x * N + y) * 2 + (1 - c), z
    me = blk(0, 0)

    own_copy = pltpu.make_async_copy(h, own, loc.at[0])
    own_copy.start()
    a_copies = []
    for half in range(2):
        a_copies.append(pltpu.make_async_copy(
            a.at[:, :, pl.ds(half * COLS, COLS)], pool.at[pl.ds((1 + half) * N * CHUNKS, N * CHUNKS)], loc.at[1 + half]
        ))
        a_copies[half].start()
    w_copy = pltpu.make_async_copy(w, held.at[me], loc.at[3])
    w_copy.start()

    barrier = pltpu.get_barrier_semaphore()
    friends = [at(1, 0), at(-1, 0), at(0, 1), at(0, -1), along(1), along(2), along(3), other]
    for friend in friends:
        pl.semaphore_signal(barrier, inc=1, device_id=friend, device_id_type=MESH)
    own_copy.wait()

    @pl.loop(0, TILES)
    def _(t):
        for i in range(UNITS // COLS):
            pool[t * CHUNKS + i // PARTS, pl.ds(i % PARTS * COLS, COLS)] = own[t, :, i * COLS:(i + 1) * COLS]

    pl.semaphore_wait(barrier, len(friends))

    sent = []

    def describe(src, dst, s, r, device):
        return pltpu.make_async_remote_copy(
            src_ref=src, dst_ref=dst, send_sem=s, recv_sem=r, device_id=device, device_id_type=MESH
        )

    def remote(src, dst, s, r, device):
        copy = describe(src, dst, s, r, device)
        copy.start()
        sent.append(copy)
        return copy

    copies = {}

    def rows_of(way, piece):
        if piece is None:
            return pl.ds(way * HALF, HALF)
        return pl.ds(way * HALF + piece * QUART, QUART)

    def place(way, first, second):
        return (first, second) if way == 0 else (second, first)

    def push(key, way, origin, piece, step, source=None):
        spot = held.at[blk(*place(way, *origin)), rows_of(way, piece)]
        i = len(copies)
        copies[key] = remote(
            spot if source is None else source.at[rows_of(way, piece)],
            spot, w_send.at[i], w_recv.at[i], at(*place(way, *step)),
        )

    def forward(way, o, sign):
        copies[(3, way, o, sign)].wait_recv()
        push((4, way, o, sign), way, (o, -sign), 0 if sign == 1 else 1, (0, sign))

    signs = (1, -1)
    for way in (0, 1):
        for sign in signs:
            push((1, way, sign), way, (0, 0), None, (sign, 0), w)
    for way in (0, 1):
        for sign in signs:
            push((3, way, 0, sign), way, (0, 0), None, (0, sign), w)

    sib_copy = remote(h, sib, s_send.at[0], s_recv.at[0], other)

    def slot_tile(holder, s):
        seen, found = jnp.int32(0), jnp.int32(0)
        for t in range(TILES):
            hit = (choice[t] == holder).astype(jnp.int32)
            found = found + jnp.where(seen == s, hit * t, 0)
            seen = seen + hit
        return found

    code = jnp.int32(0)
    for o in range(N):
        count = jnp.int32(0)
        for t in range(TILES):
            count = count + (choice[t] == o).astype(jnp.int32)
        code = code * 3 + count
    found = table[code]
    base = 81 + ((found // N) * N + (z - found % N + N) % N) * WIDTH

    def fields(entry):
        return (z + entry % 64 // 16) % N, entry // 8 % 2, jnp.minimum(entry % 8, CHUNKS - 1)

    def matrix(piece, half, k):
        return TILES * CHUNKS + (half * N + piece) * CHUNKS + k

    def z_copy(link, j):
        return describe(
            outgo.at[link, j], income.at[link, j], t_send.at[link, j], t_recv.at[link, j], along(1 - 2 * link)
        )

    def step(j, first):
        for link in range(2):
            entry = table[base + link * STEPS + j]
            piece, which, k = fields(entry)
            is_matrix = jnp.logical_and(entry >= MATRIX_KIND, entry < PASS_ON)
            value = pool[jnp.where(is_matrix, matrix(piece, which, k), slot_tile(piece, which) * CHUNKS + k)]
            if not first:
                value = lax.select(entry == PASS_ON, income[link, j - LAG], value)
            outgo[link, j] = value
            z_copy(link, j).start()

    def wide(piece):
        return jnp.concatenate([piece[i * COLS:(i + 1) * COLS] for i in range(PARTS)], axis=1)

    def matrix_rows(piece, k):
        return jnp.concatenate([pool[matrix(piece, half, k)] for half in range(2)], axis=1)

    def use(j):
        for link in range(2):
            entry = table[base + (2 + link) * STEPS + j]
            piece, which, k = fields(entry)
            got = income[link, j]
            r = jnp.dot(wide(got), matrix_rows(piece, k), preferred_element_type=F32)
            for s in range(SLOTS):
                ok = jnp.logical_and(entry // 64 == 1, which == s)
                low[s] = low[s] + lax.select(ok, r, jnp.zeros_like(r))
            rows = jnp.concatenate([wide(pool[slot_tile(piece, s) * CHUNKS + k]) for s in range(SLOTS)], axis=0)
            r = jnp.dot(rows, got, preferred_element_type=F32)
            for half in range(2):
                ok = jnp.logical_and(entry // 64 == 2, which == half)
                away[half] = away[half] + lax.select(ok, r, jnp.zeros_like(r))

    def exchange(lo, hi):
        @pl.loop(lo, hi)
        def _(j):
            for link in range(2):
                z_copy(link, j - LAG).wait_recv()
            step(j, False)
            use(j - LAG)

    def multiply(first, second):
        both = jnp.concatenate([held[first], held[second]], axis=1)
        for rows, top in ((own, 0), (sib, ROWS)):
            r = jnp.dot(rows[...].reshape(ROWS, UNITS), both, preferred_element_type=F32).astype(BF16)
            part[first, pl.ds(top, ROWS)] = r[:, :COLS]
            part[second, pl.ds(top, ROWS)] = r[:, COLS:]

    for copy in a_copies:
        copy.wait()
    for j in range(LAG):
        step(j, True)
    b_copy = pltpu.make_async_copy(b, b_v, loc.at[4])
    b_copy.start()
    away[...] = jnp.zeros_like(away)
    low[...] = jnp.zeros_like(low)
    mine = [slot_tile(z, s) for s in range(SLOTS)]

    @pl.loop(0, CHUNKS)
    def _(k):
        rows = jnp.concatenate([wide(pool[mine[s] * CHUNKS + k]) for s in range(SLOTS)], axis=0)
        r = jnp.dot(rows, matrix_rows(z, k), preferred_element_type=F32)
        for s in range(SLOTS):
            low[s] = low[s] + r[s * TILE:(s + 1) * TILE]

    exchange(LAG, 9)
    for way in (0, 1):
        for sign in signs:
            copies[(1, way, sign)].wait_recv()
            push((2, way, sign), way, (-sign, 0), 0 if sign == 1 else 1, (sign, 0))
    for way in (0, 1):
        for o in signs:
            for sign in signs:
                push((3, way, o, sign), way, (o, 0), None, (0, sign))
    for way in (0, 1):
        for sign in signs:
            forward(way, 0, sign)
    exchange(9, 11)
    w_copy.wait()
    sib_copy.wait_recv()
    multiply(blk(0, 0), blk(1, 0))
    exchange(11, 14)
    multiply(blk(0, 1), blk(0, -1))
    exchange(14, STEPS - 1)
    for link in range(2):
        z_copy(link, STEPS - 1 - LAG).wait_recv()
    use(STEPS - 1 - LAG)

    for half in range(2):
        away_send[half] = away[half].astype(BF16)
    returns = [
        remote(away_send, away_recv.at[d - 1], f_send.at[d - 1], f_recv.at[d - 1], along(d)) for d in (2, 1, 3)
    ]
    step(STEPS - 1, False)
    for way in (0, 1):
        for sign in signs:
            copies[(2, way, sign)].wait_recv()
        for sign in signs:
            push((3, way, 2, sign), way, (2, 0), None, (0, sign))
    for o in signs:
        for way in (0, 1):
            for sign in signs:
                forward(way, o, sign)
    for j in range(STEPS - LAG, STEPS):
        for link in range(2):
            z_copy(link, j).wait_recv()
        use(j)
        if j == STEPS - LAG:
            multiply(blk(-1, 0), blk(1, 1))
    for copy in returns:
        copy.wait_recv()
    flags = table[base + 4 * STEPS + 1]
    for d in (1, 2, 3):
        ok = flags // (1 << (N - d)) % 2 == 1
        for s in range(SLOTS):
            for half in range(2):
                r = away_recv[d - 1, half, s * TILE:(s + 1) * TILE].astype(F32)
                spot = low.at[s, :, half * COLS:(half + 1) * COLS]
                spot[...] = spot[...] + lax.select(ok, r, jnp.zeros_like(r))

    rank = ranks[z]
    scale = ALPHA / rank.astype(F32)
    valid = lax.broadcasted_iota(jnp.int32, (TILE, RANK), 1) < rank
    for t in range(TILES):
        slot = jnp.int32(0)
        for before in range(t):
            slot = slot + (choice[before] == choice[t]).astype(jnp.int32)
        slot = jnp.minimum(slot, SLOTS - 1)
        keep = jnp.logical_and(valid, jnp.full((TILE, RANK), choice[t], jnp.int32) == z)
        low_full[pl.ds(t * TILE, TILE)] = jnp.where(keep, low[slot], 0.0).astype(BF16)

    b_copy.wait()

    def delta(i, q):
        @pl.loop(0, N, unroll=True)
        def _(k):
            at_rows = pl.ds(pl.multiple_of((q * N + k) * 2 * COLS, 2 * COLS), 2 * COLS)
            r = lax.dot_general(
                low_full[...], b_v[at_rows], (((1,), (1,)), ((), ())), preferred_element_type=F32
            ) * scale
            r = r.astype(BF16)
            d_own[q * N + k] = lax.select(c == 0, r[:, :COLS], r[:, COLS:])
            d_send[q * N + k] = lax.select(c == 0, r[:, COLS:], r[:, :COLS])

        here = pl.ds(q * N, N)
        return remote(d_send.at[here], d_recv.at[here], s_send.at[1 + i], s_recv.at[1 + i], other)

    def role(way, dx):
        q = (x + dx + N) % N
        return ((z - q - 1) if way == 0 else (q - 1 - z)) % N

    def hop(way, block):
        b_at = blk(*block)
        return describe(
            part.at[b_at, pl.ds(way * ROWS, ROWS)], ring.at[way, b_at],
            r_send.at[way, b_at], r_recv.at[way, b_at], along(1 - 2 * way),
        )

    def finish(block):
        k = (y + block[1] + N) % N
        return describe(fin_send.at[k], fin_recv.at[k], s_send.at[5 + k], s_recv.at[5 + k], other)

    def act(way, block, turn):
        @pl.when(role(way, block[0]) == turn)
        def _():
            b_at = blk(*block)
            k = (y + block[1] + N) % N
            if turn:
                hop(way, block).wait_recv()

            @pl.loop(0, TILES)
            def _(i):
                some = pl.ds(pl.multiple_of(i * TILE, TILE), TILE)
                spot = part.at[b_at, pl.ds(pl.multiple_of(way * ROWS + i * TILE, TILE), TILE)]
                r = spot[...].astype(F32) + (d_recv if way else d_own)[b_at, some].astype(F32)
                if turn:
                    r = r + ring[way, b_at, some].astype(F32)
                r = r.astype(BF16)
                if turn < 3:
                    spot[...] = r
                elif way:
                    fin_send[k, some] = r
                else:
                    out[some, pl.ds(pl.multiple_of((2 * k + c) * COLS, COLS), COLS)] = r

            if turn < 3:
                hop(way, block).start()
            elif way:
                finish(block).start()

    order = (
        (0, 0), (1, 0), (0, 1), (0, -1), (-1, 0), (1, 1), (1, -1), (-1, 1), (-1, -1), (2, 0),
        (2, 1), (2, -1), (0, 2), (1, 2), (-1, 2), (2, 2),
    )

    def stage(turn, blocks, ways=(1, 0)):
        for block in blocks:
            for way in ways:
                act(way, block, turn)

    early, late = order[:10], order[10:]
    swaps = [delta(0, (z + 1) % N), delta(1, (z + N - 1) % N)]
    stage(0, early[:6], (0,))
    swaps[0].wait_recv()
    stage(0, early[:6], (1,))
    multiply(blk(1, -1), blk(-1, 1))
    stage(0, early[6:8])
    for way in (0, 1):
        for sign in signs:
            copies[(4, way, 0, sign)].wait_recv()
    multiply(blk(-1, -1), blk(2, 0))
    stage(0, early[8:])
    for way in (0, 1):
        for sign in signs:
            forward(way, 2, sign)
    swaps.append(delta(2, (z + 2) % N))
    swaps.append(delta(3, z))
    for copy in swaps[1:]:
        copy.wait_recv()
    stage(1, early)
    for way in (0, 1):
        for o in signs:
            for sign in signs:
                copies[(4, way, o, sign)].wait_recv()
    multiply(blk(2, 1), blk(2, -1))
    stage(0, late[:2])
    multiply(blk(0, 2), blk(1, 2))
    stage(0, late[2:4])
    stage(2, early)
    for way in (0, 1):
        for sign in signs:
            copies[(4, way, 2, sign)].wait_recv()
    multiply(blk(-1, 2), blk(2, 2))
    stage(0, late[4:])
    stage(1, late)
    stage(3, early)
    stage(2, late)
    stage(3, late)
    for block in order:
        @pl.when(role(1, block[0]) == 3)
        def _():
            k = (y + block[1] + N) % N
            finish(block).wait()
            out[:, pl.ds(pl.multiple_of((2 * k + 1 - c) * COLS, COLS), COLS)] = fin_recv[k]

        for way in (0, 1):
            @pl.when(role(way, block[0]) != 3)
            def _():
                hop(way, block).wait_send()

    @pl.loop(0, STEPS)
    def _(j):
        for link in range(2):
            z_copy(link, j).wait_send()

    for copy in sent:
        copy.wait_send()


def on_device(hidden, down_weight, choice, ranks, down, up):
    anywhere = pl.BlockSpec(memory_space=pl.ANY)
    small = pl.BlockSpec(memory_space=pltpu.SMEM)
    tiles = hidden.reshape(TILES, TILE, UNITS)
    matrix = down.reshape(N * CHUNKS, CHUNK, RANK)
    dma = pltpu.SemaphoreType.DMA
    return pl.pallas_call(
        kernel,
        out_shape=jax.ShapeDtypeStruct((ROWS, N * 2 * COLS), BF16),
        in_specs=[small, small, small, anywhere, anywhere, anywhere, anywhere],
        out_specs=pl.BlockSpec(memory_space=pltpu.VMEM),
        scratch_shapes=[
            pltpu.VMEM((N * N, UNITS, COLS), BF16),
            pltpu.VMEM((TILES, TILE, UNITS), BF16),
            pltpu.VMEM((TILES, TILE, UNITS), BF16),
            pltpu.VMEM((3 * N * CHUNKS, CHUNK, COLS), BF16),
            pltpu.VMEM((2, STEPS, CHUNK, COLS), BF16),
            pltpu.VMEM((2, STEPS, CHUNK, COLS), BF16),
            pltpu.VMEM((N * N * 2 * COLS, RANK), BF16),
            pltpu.VMEM((N * N, 2 * ROWS, COLS), BF16),
            pltpu.VMEM((N * N, ROWS, COLS), BF16),
            pltpu.VMEM((N * N, ROWS, COLS), BF16),
            pltpu.VMEM((N * N, ROWS, COLS), BF16),
            pltpu.VMEM((2, N * N, ROWS, COLS), BF16),
            pltpu.VMEM((N, ROWS, COLS), BF16),
            pltpu.VMEM((N, ROWS, COLS), BF16),
            pltpu.VMEM((SLOTS, TILE, RANK), F32),
            pltpu.VMEM((2, SLOTS * TILE, COLS), F32),
            pltpu.VMEM((2, SLOTS * TILE, COLS), BF16),
            pltpu.VMEM((N - 1, 2, SLOTS * TILE, COLS), BF16),
            pltpu.VMEM((ROWS, RANK), BF16),
            dma((5,)),
            dma((40,)),
            dma((40,)),
            dma((2, STEPS)),
            dma((2, STEPS)),
            dma((9,)),
            dma((9,)),
            dma((N - 1,)),
            dma((N - 1,)),
            dma((2, N * N)),
            dma((2, N * N)),
        ],
        compiler_params=pltpu.CompilerParams(
            collective_id=0, has_side_effects=True, vmem_limit_bytes=63 * 2**20
        ),
        cost_estimate=pl.CostEstimate(
            flops=20_000_000_000, bytes_accessed=15_000_000, transcendentals=0
        ),
    )(choice.reshape(TILES), ranks, jnp.asarray(routes()), tiles, down_weight, matrix, up[0])


def solution(mesh):
    return jax.shard_map(
        on_device,
        mesh=mesh,
        in_specs=(
            P("fsdp", "adapter"),
            P("adapter", "fsdp"),
            P("fsdp", None),
            P("fsdp"),
            P(("fsdp", "adapter"), None, None),
            P(("fsdp", "adapter"), None, None),
        ),
        out_specs=P("fsdp", "adapter"),
        check_vma=False,
    )
```
